32 devices in a mesh: shore: 4 (over x, core), cross: 8 (over z, y).
Axes of the slice: x: 2, y: 2, z: 4, core: 2. Of those that a mesh axis runs over, the one named last changes fastest.
Arguments:
- positions: float32 [2, 64, 64, 128], P(None, 'shore', 'cross'), may hold values from 0 to 1
- velocity: float32 [2, 64, 64, 128], P(None, 'shore', 'cross'), may hold values from -3 to 3
- density: float32 [64, 64, 128], P('shore', 'cross'), may hold values from 0.97 to 1.03
- particle_mass: float32 [64, 64, 128], P('shore', 'cross'), may hold values from 0.004 to 0.016
- cell_count: int32 [64, 64], P('shore', 'cross'), may hold values from 0 to 128
- wind_seed: int32 [64, 64, 128], P('shore', 'cross'), may hold values from 0 to 15
- wind_table: float32 [2, 16], replicated, may hold values from -4 to 4
- migrant_slot: int32 [4, 8, 4, 1792], P('shore', 'cross'), may hold values from 0 to 16383
- migrant_count: int32 [4, 8, 4], P('shore', 'cross'), may hold values from 896 to 1792, as said below
Outputs:
- state_next: float32 [7, 64, 64, 128], P(None, 'shore', 'cross')
- arrivals: float32 [4, 8, 4, 8, 1792], P('shore', 'cross')
The draws below stay inside these ranges and needn't reach their ends.
Inputs may be any that keep to these rules, and one draw needn't show every extreme that they name: `migrant_slot`: a slot in one device's own blocks, numbered (block along * 8 + block across) * 128 + slot. `migrant_count`: on every device, at least one direction has exactly 1792 migrants.
All inputs are finite; a program needn't handle non-finite values.
Results may differ from the reference program's by a relative error of at most 0.0003.
Values sent between devices are 32-bit elements; how exact they have to be, the bound alone decides.
No kernel may reach another device: no remote copies, remote signals or barrier semaphores. Data moves between devices by JAX's collectives and lax.ppermute only.
A program may use at most 64 MiB of HBM per device.

```python
import math
import jax
import jax.numpy as jnp
from jax import lax

CX = 16
CY = 8
P_SIZE = 128
LEVELS = 16
MIG = 1792
NCX = 64
NCY = 64
N_SHORE = 4
N_CROSS = 8


def draw_migrant_count(key, part):
    base = jax.random.randint(jax.random.fold_in(key, 11), (N_SHORE, N_CROSS, 4), MIG // 2, MIG + 1)
    full_dir = jax.random.randint(jax.random.fold_in(key, 12), (N_SHORE, N_CROSS, 1), 0, 4)
    directions = jnp.arange(4, dtype=jnp.int32)[None, None, :]
    return jnp.where(directions == full_dir, MIG, base).astype(jnp.int32)


def draw_cell_count(key, part):
    dense = jax.random.randint(jax.random.fold_in(key, 21), (NCX, NCY), P_SIZE // 2, P_SIZE + 1)
    sparse = jax.random.randint(jax.random.fold_in(key, 22), (NCX, NCY), 0, P_SIZE // 8 + 1)
    shore_device = jnp.arange(NCX, dtype=jnp.int32) // CX
    thin_reach = (shore_device >= N_SHORE - N_SHORE // 3)[:, None]
    return jnp.where(thin_reach, sparse, dense).astype(jnp.int32)


def place_ends(values, stream_key, smallest, top_value):
    longest = values.shape.index(max(values.shape))
    spots = []
    for shift in (0, 1):
        where = [jax.random.randint(jax.random.fold_in(stream_key, axis), (), 0, length) for axis, length in enumerate(values.shape)]
        where[longest] = (where[longest] + shift) % values.shape[longest]
        spots.append(tuple(where))
    return values.at[spots[0]].set(smallest).at[spots[1]].set(top_value)


def block_levels(own_key, dims, split, low, largest):
    gain = 1.0
    for dim, blocks in split:
        steps = jax.random.uniform(jax.random.fold_in(jax.random.fold_in(own_key, 6), dim), (blocks,), jnp.float32, low / len(split), largest / len(split))
        gain = gain * jnp.repeat(jnp.exp(steps), dims[dim] // blocks).reshape((-1,) + (1,) * (len(dims) - 1 - dim))
    return gain


def scatter_about(key, extent, scale, bound, shards=(), held_as=jnp.bfloat16):
    array = jax.random.normal(key, extent, jnp.float32) * scale
    if len(shards) > 0:
        array = block_levels(key, extent, shards, -0.22, 0.18) * array
    return jnp.clip(array, min=-bound, max=bound).astype(held_as)


def setup_inputs(seed: int = 0) -> dict:
    keys = jax.random.split(jax.random.key(seed), 10)
    positions = jnp.clip(1.0 * jax.random.uniform(keys[0], (2, NCX, NCY, P_SIZE), jnp.float32) ** block_levels(keys[0], (2, NCX, NCY, P_SIZE), ((1, 4), (2, 8)), -0.2, 0.2), 0.0, 1.0)
    velocity = scatter_about(keys[1], (2, NCX, NCY, P_SIZE), 0.5, 3.0, ((1, 4), (2, 8)), jnp.float32)
    density = jnp.clip(0.97 + 0.059999943 * jax.random.uniform(keys[2], (NCX, NCY, P_SIZE), jnp.float32) ** block_levels(keys[2], (NCX, NCY, P_SIZE), ((0, 4), (1, 8)), -0.2, 0.2), 0.97, 1.03)
    particle_mass = jnp.clip(jnp.exp(math.log(0.016) - 1.3862944 * jax.random.uniform(keys[3], (NCX, NCY, P_SIZE), jnp.float32) ** block_levels(keys[3], (NCX, NCY, P_SIZE), ((0, 4), (1, 8)), -0.2, 0.2)), 0.004, 0.016)
    cell_count = draw_cell_count(jax.random.fold_in(keys[9], 71), 0)
    wind_seed = place_ends(jax.random.randint(keys[5], (NCX, NCY, P_SIZE), 0, LEVELS), jax.random.fold_in(keys[5], 1), 0, LEVELS - 1).astype(jnp.int32)
    wind_table = scatter_about(keys[6], (2, LEVELS), 1.0, 4.0, (), jnp.float32)
    migrant_slot = place_ends(jax.random.randint(keys[7], (N_SHORE, N_CROSS, 4, MIG), 0, CX * CY * P_SIZE), jax.random.fold_in(keys[7], 1), 0, (CX * CY * P_SIZE) - 1).astype(jnp.int32)
    migrant_count = draw_migrant_count(jax.random.fold_in(keys[9], 71), 0)
    return dict(positions=positions, velocity=velocity, density=density, particle_mass=particle_mass, cell_count=cell_count, wind_seed=wind_seed, wind_table=wind_table, migrant_slot=migrant_slot, migrant_count=migrant_count)


sound_speed = 10.0
smooth = 0.5
viscous = 0.1
kernel_norm = 7.0 / (4.0 * 3.141592653589793 * smooth * smooth)
grad_coef = -5.0 * kernel_norm / (smooth * smooth)

def pressure_ratio(density):
    cube = density * density * density
    seventh = cube * cube * density
    pressure = sound_speed * sound_speed / 7.0 * (seventh - 1.0)
    return pressure / (density * density)

def pack_fields(positions, velocity, density, particle_mass, live_slots):
    return jnp.stack([positions[0], positions[1], velocity[0], velocity[1], density, particle_mass, live_slots, pressure_ratio(density)])

def tile_terms(own_cells, near_cells, step_x, step_y):
    offset_x = own_cells[0][:, :, None] - near_cells[0][:, None, :] - step_x
    offset_y = own_cells[1][:, :, None] - near_cells[1][:, None, :] - step_y
    dist_sq = offset_x * offset_x + offset_y * offset_y
    radius = jnp.sqrt(dist_sq) / smooth
    falloff = jnp.maximum(1.0 - 0.5 * radius, 0.0)
    gradient = grad_coef * falloff * falloff * falloff
    relative_u = own_cells[2][:, :, None] - near_cells[2][:, None, :]
    relative_v = own_cells[3][:, :, None] - near_cells[3][:, None, :]
    approach = relative_u * offset_x + relative_v * offset_y
    viscous_mu = smooth * jnp.minimum(approach, 0.0) / (dist_sq + 0.01 * smooth * smooth)
    mean_density = 0.5 * (own_cells[4][:, :, None] + near_cells[4][:, None, :])
    visc_term = -viscous * sound_speed * viscous_mu / mean_density
    weighted = (near_cells[5] * near_cells[6])[:, None, :] * gradient
    coupling = weighted * (own_cells[7][:, :, None] + near_cells[7][:, None, :] + visc_term)
    force_x = -lax.optimization_barrier(jnp.sum(coupling * offset_x, axis=2))
    force_y = -lax.optimization_barrier(jnp.sum(coupling * offset_y, axis=2))
    density_rate = lax.optimization_barrier(jnp.sum(weighted * approach, axis=2))
    return jnp.stack([force_x, force_y, density_rate])

def row_forces(three_rows):
    own_cells = three_rows[:, 1, 1:-1]
    width = own_cells.shape[1]
    summed = jnp.zeros((3,) + own_cells.shape[1:], jnp.float32)
    for step_x in (-1, 0, 1):
        for step_y in (-1, 0, 1):
            near_cells = three_rows[:, 1 + step_x, 1 + step_y:1 + step_y + width]
            summed = summed + tile_terms(own_cells, near_cells, float(step_x), float(step_y))
    return summed

def all_forces(extended):
    row_count = extended.shape[1] - 2

    def one_row(row_index):
        return row_forces(lax.dynamic_slice_in_dim(extended, row_index, 3, 1))
    computed = lax.map(one_row, jnp.arange(row_count, dtype=jnp.int32))
    return jnp.transpose(computed, (1, 0, 2, 3))

def time_step(peak_acc, peak_speed):
    return 0.25 * smooth / (sound_speed + peak_speed + jnp.sqrt(smooth * peak_acc))

def pick_migrants(flattened, slot_list, live_count):
    width = slot_list.shape[1]
    picked = jnp.take(flattened, slot_list.reshape(-1).astype(jnp.int32), axis=1)
    picked = jnp.transpose(picked.reshape(flattened.shape[0], 4, width), (1, 0, 2))
    live_rows = (jnp.arange(width, dtype=jnp.int32)[None, :] < live_count[:, None]).astype(jnp.float32)
    return picked * live_rows[:, None, :]

def reference(positions, velocity, density, particle_mass, cell_count, wind_seed, wind_table, migrant_slot, migrant_count):
    slot_ids = jnp.arange(P_SIZE, dtype=jnp.int32)
    live_slots = (slot_ids[None, None, :] < cell_count[:, :, None]).astype(jnp.float32)
    fields = pack_fields(positions, velocity, density, particle_mass, live_slots)
    extended = jnp.pad(fields, ((0, 0), (1, 1), (1, 1), (0, 0)))
    forces = all_forces(extended)
    windage = wind_table[:, wind_seed]
    acceleration = (forces[:2] + windage) * live_slots[None]
    density_rate = forces[2] * live_slots
    peak_acc = jnp.max(jnp.sqrt(acceleration[0] * acceleration[0] + acceleration[1] * acceleration[1]))
    peak_speed = jnp.max(jnp.sqrt(velocity[0] * velocity[0] + velocity[1] * velocity[1]) * live_slots)
    delta_t = time_step(peak_acc, peak_speed)
    new_velocity = (velocity + delta_t * acceleration) * live_slots[None]
    new_position = (positions + delta_t * new_velocity) * live_slots[None]
    new_density = (density + delta_t * density_rate) * live_slots
    state_next = jnp.concatenate([new_position, new_velocity, new_density[None], acceleration])
    carried = jnp.concatenate([new_position, new_velocity, new_density[None], (particle_mass * live_slots)[None], acceleration])
    per_device = carried.reshape(8, N_SHORE, CX, N_CROSS, CY, P_SIZE)
    per_device = jnp.transpose(per_device, (1, 3, 0, 2, 4, 5)).reshape(N_SHORE, N_CROSS, 8, CX * CY * P_SIZE)
    leaving = jax.vmap(jax.vmap(pick_migrants))(per_device, migrant_slot, migrant_count)
    zero_shore = jnp.zeros_like(leaving[:1, :, 0])
    eastward = jnp.concatenate([zero_shore, leaving[:-1, :, 0]], axis=0)
    westward = jnp.concatenate([leaving[1:, :, 1], zero_shore], axis=0)
    zero_cross = jnp.zeros_like(leaving[:, :1, 2])
    northward = jnp.concatenate([zero_cross, leaving[:, :-1, 2]], axis=1)
    southward = jnp.concatenate([leaving[:, 1:, 3], zero_cross], axis=1)
    arrivals = jnp.stack([eastward, westward, northward, southward], axis=2)
    return (state_next, arrivals)
```

```python
import functools

import jax
import jax.numpy as jnp
import numpy as np
from jax import lax
from jax.experimental import pallas as pl
from jax.experimental.pallas import tpu as pltpu
from jax.sharding import PartitionSpec as P

sound_speed = 10.0
smooth = 0.5
kernel_norm = 7.0 / (4.0 * 3.141592653589793 * smooth * smooth)
grad_coef = -5.0 * kernel_norm / (smooth * smooth)
f32 = jnp.float32
SUB = 8
GRAN = 2
VMEM_LIMIT = 48 * 1024 * 1024


def passed_along(array, axis, by):
    peers = lax.axis_size(axis)
    pairs = [(i, i + by) for i in range(peers) if 0 <= i + by < peers]
    return lax.ppermute(array, axis, pairs)


def everywhere_max(array):
    for axis in ("cross", "shore"):
        peers = lax.axis_size(axis)
        step = 1
        while step < peers:
            if peers & (peers - 1) == 0:
                pairs = [(i, i ^ step) for i in range(peers)]
            else:
                pairs = [(i, (i + step) % peers) for i in range(peers)]
            array = jnp.maximum(array, lax.ppermute(array, axis, pairs))
            step *= 2
    return array


def pressure_ratio(density):
    cube = density * density * density
    seventh = cube * cube * density
    pressure = sound_speed * sound_speed / 7.0 * (seventh - 1.0)
    return pressure / (density * density)


def pair_terms(own, near):
    dx = own[0] - near[0]
    dy = own[1] - near[1]
    dist_sq = dx * dx + dy * dy
    guarded = jnp.maximum(dist_sq, 1e-30)
    radius = guarded * lax.rsqrt(guarded)
    falloff = jnp.maximum(1.0 - radius, 0.0)
    weight = (falloff * falloff) * (falloff * (own[6] * near[6]))
    approach = (own[2] - near[2]) * dx + (own[3] - near[3]) * dy
    bottom = (dist_sq + 0.01 * smooth * smooth) * (own[4] + near[4])
    total = (own[5] + near[5]) - jnp.minimum(approach, 0.0) * pltpu.reciprocal(bottom, approx=True)
    shared = weight * total
    return shared * dx, shared * dy, weight * approach


def plus(total, term):
    return term if total is None else tuple(a + b for a, b in zip(total, term))


def center_tiles(q_ref, behind_ref, acc_ref, rows_ref, center, tiles, near):
    columns = jnp.transpose(q_ref[center])
    lanes = columns.shape[0]
    others = []
    for block, step_x, step_y, _ in near:
        fields = [q_ref[block, k : k + 1, :] for k in range(7)]
        fields[0] = fields[0] + step_x
        fields[1] = fields[1] + step_y
        others.append([jnp.broadcast_to(f, (SUB, lanes)) for f in fields])
    sums = [None] * len(near)
    both = any(two for _, _, _, two in near)
    for t in range(tiles):
        tile = columns[SUB * t : SUB * t + SUB]
        mine = [jnp.broadcast_to(tile[:, k : k + 1], (SUB, lanes)) for k in range(7)]
        behind = None
        for n in range(len(near)):
            term = pair_terms(others[n], mine)
            sums[n] = plus(sums[n], term)
            if near[n][3]:
                behind = plus(behind, term)
        if both:
            for k in range(3):
                behind_ref[k, SUB * t : SUB * t + SUB, :] = behind[k]
    for n in range(len(near)):
        for k in range(3):
            acc_ref[near[n][0], k] = acc_ref[near[n][0], k] + sums[n][k]
    if both:
        ones = jnp.ones((16, lanes), jnp.bfloat16)
        dims = (((1,), (1,)), ((), ()))
        sub = lax.broadcasted_iota(jnp.int32, (SUB, lanes), 0)
        total = jnp.zeros((SUB, lanes), f32)
        for k in range(3):
            part = behind_ref[k]
            high = part.astype(jnp.bfloat16)
            rest = part - high.astype(f32)
            mid = rest.astype(jnp.bfloat16)
            low = (rest - mid.astype(f32)).astype(jnp.bfloat16)
            row = sum(
                lax.dot_general(ones, piece, dims, preferred_element_type=f32)
                for piece in (high, mid, low)
            )
            total = jnp.where(sub == k, row[:SUB], total)
        rows_ref[center] = total


def center_block(q_ref, behind_ref, acc_ref, rows_ref, center, count, near):
    most = q_ref.shape[2] // SUB
    tiles = pl.cdiv(count, SUB * GRAN)
    for v in range(1, most // GRAN + 1):

        @pl.when(tiles == v)
        def _():
            center_tiles(q_ref, behind_ref, acc_ref, rows_ref, center, v * GRAN, near)


def own_kernel(count_ref, q_ref, out_ref, acc_ref, behind_ref, *, rows, cols):
    blocks = rows * cols
    lanes = q_ref.shape[2]

    def clear(b, _):
        acc_ref[b] = jnp.zeros((3, SUB, lanes), f32)
        out_ref[b] = jnp.zeros((SUB, lanes), f32)
        return 0

    lax.fori_loop(0, blocks, clear, 0)
    behind_ref[...] = jnp.zeros(behind_ref.shape, f32)

    def run(r, c, steps):
        center = r * cols + c
        near = [(center + sx * cols + sy, float(sx), float(sy), (sx, sy) != (0, 0)) for sx, sy in steps]
        center_block(q_ref, behind_ref, acc_ref, out_ref, center, count_ref[center], near)

    def one_row(r, _):
        run(r, 0, [(0, 1), (1, 0), (1, 1), (0, 0)])

        def middle(c, _):
            run(r, c, [(0, 1), (1, -1), (1, 0), (1, 1), (0, 0)])
            return 0

        lax.fori_loop(1, cols - 1, middle, 0)
        run(r, cols - 1, [(1, -1), (1, 0), (0, 0)])
        return 0

    lax.fori_loop(0, rows - 1, one_row, 0)

    def last_row(c, _):
        run(rows - 1, c, [(0, 1), (0, 0)])
        return 0

    lax.fori_loop(0, cols - 1, last_row, 0)
    run(rows - 1, cols - 1, [(0, 0)])
    sub = lax.broadcasted_iota(jnp.int32, (SUB, lanes), 0)

    def close(b, _):
        part = acc_ref[b]
        rows_sum = [jnp.sum(part[k], axis=0, keepdims=True) for k in range(3)]
        front = jnp.concatenate(rows_sum + [jnp.zeros((SUB - 3, lanes), f32)], axis=0)
        behind = out_ref[b]
        out_ref[b] = jnp.where(sub == 2, front + behind, front - behind)
        return 0

    lax.fori_loop(0, blocks, close, 0)


def halo_kernel(count_ref, index_ref, step_ref, q_ref, own_ref, wind_ref, out_ref, peak_ref, acc_ref, *, rows, cols):
    lanes = q_ref.shape[2]

    def clear(b, _):
        acc_ref[b] = jnp.zeros((3, SUB, lanes), f32)
        return 0

    lax.fori_loop(0, (rows + 2) * (cols + 2), clear, 0)

    def one_center(n, _):
        center = index_ref[4 * n]
        near = [
            (index_ref[4 * n + 1 + k], step_ref[6 * n + 2 * k], step_ref[6 * n + 2 * k + 1], False)
            for k in range(3)
        ]
        center_block(q_ref, None, acc_ref, None, center, count_ref[center], near)
        return 0

    lax.fori_loop(0, 2 * (rows + cols + 2), one_center, 0)
    peak_ref[...] = jnp.zeros(peak_ref.shape, f32)

    def close_row(r, _):
        def close(c, _):
            b = r * cols + c
            e = (r + 1) * (cols + 2) + c + 1
            part = acc_ref[e]
            total = [jnp.sum(part[k], axis=0, keepdims=True) + own_ref[b, k : k + 1, :] for k in range(3)]
            mass = q_ref[e, 6:7, :]
            live = mass > 0.0
            scale = grad_coef / jnp.where(live, mass, 1.0)
            here = pl.ds(b, 1)
            acc_x = jnp.where(live, wind_ref[0, here, :] - scale * total[0], 0.0)
            acc_y = jnp.where(live, wind_ref[1, here, :] - scale * total[1], 0.0)
            out_ref[0, here, :] = acc_x
            out_ref[1, here, :] = acc_y
            out_ref[2, here, :] = jnp.where(live, scale * total[2], 0.0)
            peak_ref[0:1] = jnp.maximum(peak_ref[0:1], acc_x * acc_x + acc_y * acc_y)
            return 0

        lax.fori_loop(0, cols, close, 0)
        return 0

    lax.fori_loop(0, rows, close_row, 0)


def halo_lists(rows, cols):
    wide = cols + 2
    index, step = [], []

    def add(r, c, steps):
        index.extend([r * wide + c] + [(r + sx) * wide + c + sy for sx, sy in steps])
        for sx, sy in steps:
            step.extend([sx, sy])

    for c in range(wide):
        add(0, c, [(1, -1), (1, 0), (1, 1)])
        add(rows + 1, c, [(-1, -1), (-1, 0), (-1, 1)])
    for r in range(1, rows + 1):
        add(r, 0, [(-1, 1), (0, 1), (1, 1)])
        add(r, cols + 1, [(-1, -1), (0, -1), (1, -1)])
    return np.asarray(index, np.int32), np.asarray(step, np.float32)


def spaces(smem, vmem):
    return [pl.BlockSpec(memory_space=pltpu.SMEM)] * smem + [pl.BlockSpec(memory_space=pltpu.VMEM)] * vmem


def own_forces(counts, fields, rows, cols):
    blocks, _, lanes = fields.shape
    return pl.pallas_call(
        functools.partial(own_kernel, rows=rows, cols=cols),
        out_shape=jax.ShapeDtypeStruct((blocks, SUB, lanes), f32),
        in_specs=spaces(1, 1),
        out_specs=pl.BlockSpec(memory_space=pltpu.VMEM),
        scratch_shapes=[pltpu.VMEM((blocks, 3, SUB, lanes), f32), pltpu.VMEM((3, lanes, lanes), f32)],
        compiler_params=pltpu.CompilerParams(vmem_limit_bytes=VMEM_LIMIT),
        cost_estimate=pl.CostEstimate(flops=400_000_000, bytes_accessed=2_000_000, transcendentals=20_000_000),
    )(counts, fields)


def halo_forces(counts, extended, own, wind, rows, cols):
    blocks = rows * cols
    lanes = extended.shape[2]
    index, step = halo_lists(rows, cols)
    return pl.pallas_call(
        functools.partial(halo_kernel, rows=rows, cols=cols),
        out_shape=(
            jax.ShapeDtypeStruct((3, blocks, lanes), f32),
            jax.ShapeDtypeStruct((SUB, lanes), f32),
        ),
        in_specs=spaces(3, 3),
        out_specs=tuple(spaces(0, 2)),
        scratch_shapes=[pltpu.VMEM(((rows + 2) * (cols + 2), 3, SUB, lanes), f32)],
        compiler_params=pltpu.CompilerParams(vmem_limit_bytes=VMEM_LIMIT),
    )(counts, jnp.asarray(index), jnp.asarray(step), extended, own, wind)


def pick_kernel(slot_ref, keep_ref, table_ref, out_ref):
    count, blocks, lanes = table_ref.shape
    for g in range(slot_ref.shape[0] // SUB):
        here = slice(g * SUB, g * SUB + SUB)
        slots = slot_ref[here]
        block_of = slots // lanes
        lane_of = slots % lanes

        def one(b, picked):
            hit = block_of == b
            rows = [jnp.broadcast_to(table_ref[k, pl.ds(b, 1), :], (SUB, lanes)) for k in range(count)]
            got = [jnp.take_along_axis(row, lane_of, axis=1) for row in rows]
            return tuple(jnp.where(hit, new, old) for new, old in zip(got, picked))

        start = (jnp.zeros((SUB, lanes), f32),) * count
        picked = lax.fori_loop(0, blocks, one, start, unroll=8)
        for k in range(count):
            out_ref[k, here] = picked[k] * keep_ref[here]


def pick(slots, keep, table, ways):
    count = table.shape[0]
    rows, lanes = slots.shape
    picked = pl.pallas_call(
        pick_kernel,
        out_shape=jax.ShapeDtypeStruct((count, rows, lanes), f32),
        in_specs=spaces(0, 3),
        out_specs=pl.BlockSpec(memory_space=pltpu.VMEM),
        compiler_params=pltpu.CompilerParams(vmem_limit_bytes=VMEM_LIMIT),
    )(slots, keep, table)
    return picked.reshape(count, ways, rows // ways, lanes)


def send_on(picked):
    return [
        passed_along(picked[:, 0], "shore", 1),
        passed_along(picked[:, 1], "shore", -1),
        passed_along(picked[:, 2], "cross", 1),
        passed_along(picked[:, 3], "cross", -1),
    ]


def time_step(peak_acc, peak_speed):
    return 0.25 * smooth / (sound_speed + peak_speed + jnp.sqrt(smooth * peak_acc))


def body(
    positions,
    velocity,
    density,
    particle_mass,
    cell_count,
    wind_seed,
    wind_table,
    migrant_slot,
    migrant_count,
):
    _, rows, cols, lanes = positions.shape
    blocks = rows * cols
    slot_ids = jnp.arange(lanes, dtype=jnp.int32)
    alive = slot_ids[None, None, :] < cell_count[:, :, None]
    live = alive.astype(f32)
    live_mass = particle_mass * live
    fields = jnp.stack(
        [
            positions[0],
            positions[1],
            velocity[0],
            velocity[1],
            density,
            pressure_ratio(density),
            live_mass,
            live,
        ],
        axis=2,
    )
    above = passed_along(fields[rows - 1 :], "shore", 1)
    below = passed_along(fields[:1], "shore", -1)
    tall = jnp.concatenate([above, fields, below], axis=0)
    left = passed_along(tall[:, cols - 1 :], "cross", 1)
    right = passed_along(tall[:, :1], "cross", -1)
    extended = jnp.concatenate([left, tall, right], axis=1)
    extended = extended.reshape((rows + 2) * (cols + 2), SUB, lanes)
    wide_count = jnp.sum(extended[:, 7] > 0.0, axis=1, dtype=jnp.int32)

    own = own_forces(cell_count.reshape(-1), fields.reshape(blocks, SUB, lanes), rows, cols)

    level_ids = jnp.arange(wind_table.shape[1], dtype=jnp.int32)
    one_hot = (wind_seed[None] == level_ids[:, None, None, None]).astype(f32)
    windage = jnp.einsum("cl,lxyp->cxyp", wind_table, one_hot, precision=lax.Precision.HIGHEST)

    ways = migrant_slot.shape[2]
    width = migrant_slot.shape[3]
    slots = migrant_slot.reshape(-1, lanes)
    keep = jnp.arange(width, dtype=jnp.int32)[None, :] < migrant_count.reshape(ways, 1)
    keep = keep.astype(f32).reshape(-1, lanes)
    early = jnp.stack(
        [
            positions[0] * live,
            positions[1] * live,
            velocity[0] * live,
            velocity[1] * live,
            density * live,
            live_mass,
        ]
    )
    came_early = send_on(pick(slots, keep, early.reshape(-1, blocks, lanes), ways))

    late, peak = halo_forces(
        wide_count, extended, own, windage.reshape(2, blocks, lanes), rows, cols
    )
    speed_sq = velocity[0] * velocity[0] + velocity[1] * velocity[1]
    peaks = jnp.stack([jnp.max(peak), jnp.max(speed_sq * live)])
    peaks = jnp.sqrt(everywhere_max(peaks))
    delta_t = time_step(peaks[0], peaks[1])
    came_late = send_on(pick(slots, keep, late, ways))

    acceleration = late[:2].reshape(2, rows, cols, lanes)
    rate = late[2].reshape(rows, cols, lanes)
    new_velocity = (velocity + delta_t * acceleration) * live[None]
    new_position = (positions + delta_t * new_velocity) * live[None]
    new_density = (density + delta_t * rate) * live
    state_next = jnp.concatenate([new_position, new_velocity, new_density[None], acceleration])

    at = jnp.stack(came_early)
    on = jnp.stack(came_late)
    moved_velocity = at[:, 2:4] + delta_t * on[:, 0:2]
    moved_position = at[:, 0:2] + delta_t * moved_velocity
    moved_density = at[:, 4:5] + delta_t * on[:, 2:3]
    arrivals = jnp.concatenate(
        [moved_position, moved_velocity, moved_density, at[:, 5:6], on[:, 0:2]], axis=1
    )
    return (state_next, arrivals.reshape(1, 1, ways, arrivals.shape[1], width))


def solution(mesh):
    in_specs = (
        P(None, "shore", "cross", None),
        P(None, "shore", "cross", None),
        P("shore", "cross", None),
        P("shore", "cross", None),
        P("shore", "cross"),
        P("shore", "cross", None),
        P(),
        P("shore", "cross", None, None),
        P("shore", "cross", None),
    )
    out_specs = (P(None, "shore", "cross", None), P("shore", "cross", None, None, None))
    return jax.shard_map(body, mesh=mesh, in_specs=in_specs, out_specs=out_specs, check_vma=False)
```

```python
import functools

import jax
import jax.numpy as jnp
import numpy as np
from jax import lax
from jax.experimental import pallas as pl
from jax.experimental.pallas import tpu as pltpu
from jax.sharding import PartitionSpec as P

sound_speed = 10.0
smooth = 0.5
kernel_norm = 7.0 / (4.0 * 3.141592653589793 * smooth * smooth)
grad_coef = -5.0 * kernel_norm / (smooth * smooth)
f32 = jnp.float32
SUB = 8
GRAN = 2
VMEM_LIMIT = 48 * 1024 * 1024


def passed_along(array, axis, by):
    peers = lax.axis_size(axis)
    pairs = [(i, i + by) for i in range(peers) if 0 <= i + by < peers]
    return lax.ppermute(array, axis, pairs)


def everywhere_max(array):
    for axis in ("cross", "shore"):
        peers = lax.axis_size(axis)
        step = 1
        while step < peers:
            if peers & (peers - 1) == 0:
                pairs = [(i, i ^ step) for i in range(peers)]
            else:
                pairs = [(i, (i + step) % peers) for i in range(peers)]
            array = jnp.maximum(array, lax.ppermute(array, axis, pairs))
            step *= 2
    return array


def pressure_ratio(density):
    cube = density * density * density
    seventh = cube * cube * density
    pressure = sound_speed * sound_speed / 7.0 * (seventh - 1.0)
    return pressure / (density * density)


def pair_terms(own, near):
    dx = own[0] - near[0]
    dy = own[1] - near[1]
    dist_sq = dx * dx + dy * dy
    guarded = jnp.maximum(dist_sq, 1e-30)
    radius = guarded * lax.rsqrt(guarded)
    falloff = jnp.maximum(1.0 - radius, 0.0)
    weight = (falloff * falloff) * (falloff * (own[6] * near[6]))
    approach = (own[2] - near[2]) * dx + (own[3] - near[3]) * dy
    bottom = (dist_sq + 0.01 * smooth * smooth) * (own[4] + near[4])
    total = (own[5] + near[5]) - jnp.minimum(approach, 0.0) * pltpu.reciprocal(bottom, approx=True)
    shared = weight * total
    return shared * dx, shared * dy, weight * approach


def plus(total, term):
    return term if total is None else tuple(a + b for a, b in zip(total, term))


def center_tiles(q_ref, columns_ref, behind_ref, acc_ref, rows_ref, center, tiles, near, before):
    lanes = q_ref.shape[2]
    if before is not None:
        close_behind(behind_ref, rows_ref, before)
    others = []
    for block, _, step_x, step_y, _ in near:
        fields = [q_ref[block, k : k + 1, :] for k in range(7)]
        fields[0] = fields[0] + step_x
        fields[1] = fields[1] + step_y
        others.append([jnp.broadcast_to(f, (SUB, lanes)) for f in fields])
    sums = [None] * len(near)
    for t in range(tiles):
        tile = columns_ref[center, SUB * t : SUB * t + SUB, 0:SUB]
        mine = [jnp.broadcast_to(tile[:, k : k + 1], (SUB, lanes)) for k in range(7)]
        behind = None
        for n in range(len(near)):
            term = pair_terms(others[n], mine)
            sums[n] = plus(sums[n], term)
            if near[n][4]:
                behind = plus(behind, term)
        if behind is not None:
            for k in range(3):
                behind_ref[k, SUB * t : SUB * t + SUB, :] = behind[k]
    for n in range(len(near)):
        for k in range(3):
            acc_ref[near[n][1], k] = acc_ref[near[n][1], k] + sums[n][k]


def close_behind(behind_ref, rows_ref, center):
    lanes = behind_ref.shape[2]
    ones = jnp.ones((16, lanes), jnp.bfloat16)
    dims = (((1,), (1,)), ((), ()))
    sub = lax.broadcasted_iota(jnp.int32, (SUB, lanes), 0)
    total = jnp.zeros((SUB, lanes), f32)
    for k in range(3):
        part = behind_ref[k]
        high = part.astype(jnp.bfloat16)
        low = (part - high.astype(f32)).astype(jnp.bfloat16)
        row = sum(
            lax.dot_general(ones, piece, dims, preferred_element_type=f32) for piece in (high, low)
        )
        total = jnp.where(sub == k, row[:SUB], total)
    rows_ref[center] = total


def center_block(q_ref, columns_ref, behind_ref, acc_ref, rows_ref, center, count, near, before):
    most = q_ref.shape[2] // SUB
    tiles = pl.cdiv(count, SUB * GRAN)
    for v in range(0 if before is not None else 1, most // GRAN + 1):

        @pl.when(tiles == v)
        def _():
            if v == 0:
                close_behind(behind_ref, rows_ref, before)
                behind_ref[...] = jnp.zeros(behind_ref.shape, f32)
            else:
                center_tiles(
                    q_ref, columns_ref, behind_ref, acc_ref, rows_ref, center, v * GRAN, near, before
                )


def turn_columns(q_ref, columns_ref, blocks):
    def turn(b, _):
        columns_ref[b, :, 0:SUB] = jnp.transpose(q_ref[b])
        return 0

    lax.fori_loop(0, blocks, turn, 0, unroll=4)


def own_kernel(
    count_ref, pos_ref, vel_ref, rho_ref, mass_ref, out_ref, q_ref, acc_ref, columns_ref, behind_ref, *, rows, cols
):
    blocks = rows * cols
    lanes = q_ref.shape[2]
    flat = q_ref.reshape(blocks * SUB, lanes)

    def fill(g, _):
        here = pl.ds(pl.multiple_of(g * SUB, SUB), SUB)
        density = rho_ref[here, :]
        values = [
            pos_ref[0, here, :],
            pos_ref[1, here, :],
            vel_ref[0, here, :],
            vel_ref[1, here, :],
            density,
            pressure_ratio(density),
            mass_ref[here, :],
            density,
        ]
        for k in range(SUB):
            flat[pl.ds(g * SUB * SUB + k, SUB, stride=SUB), :] = values[k]
        return 0

    lax.fori_loop(0, blocks // SUB, fill, 0)

    def clear(b, _):
        acc_ref[b] = jnp.zeros((3, SUB, lanes), f32)
        return 0

    lax.fori_loop(0, blocks, clear, 0, unroll=4)
    behind_ref[...] = jnp.zeros(behind_ref.shape, f32)
    turn_columns(q_ref, columns_ref, blocks)

    def run(r, c, steps):
        center = r * cols + c
        near = [
            (center + sx * cols + sy, center + sx * cols + sy, float(sx), float(sy), (sx, sy) != (0, 0))
            for sx, sy in steps
        ]
        center_block(
            q_ref, columns_ref, behind_ref, acc_ref, out_ref, center, count_ref[center], near,
            jnp.maximum(center - 1, 0),
        )

    def one_row(r, _):
        run(r, 0, [(0, 1), (1, 0), (1, 1), (0, 0)])

        def middle(c, _):
            run(r, c, [(0, 1), (1, -1), (1, 0), (1, 1), (0, 0)])
            return 0

        lax.fori_loop(1, cols - 1, middle, 0)
        run(r, cols - 1, [(1, -1), (1, 0), (0, 0)])
        return 0

    lax.fori_loop(0, rows - 1, one_row, 0)

    def last_row(c, _):
        run(rows - 1, c, [(0, 1), (0, 0)])
        return 0

    lax.fori_loop(0, cols - 1, last_row, 0)
    run(rows - 1, cols - 1, [(0, 0)])
    out_ref[blocks - 1] = jnp.zeros((SUB, lanes), f32)
    sub = lax.broadcasted_iota(jnp.int32, (SUB, lanes), 0)

    def close(b, _):
        part = acc_ref[b]
        rows_sum = [jnp.sum(part[k], axis=0, keepdims=True) for k in range(3)]
        front = jnp.concatenate(rows_sum + [jnp.zeros((SUB - 3, lanes), f32)], axis=0)
        behind = out_ref[b]
        out_ref[b] = jnp.where(sub == 2, front + behind, front - behind)
        return 0

    lax.fori_loop(0, blocks, close, 0, unroll=4)


def halo_kernel(
    count_ref, index_ref, step_ref, halo_ref, q_ref, own_ref, wind_ref, out_ref, peak_ref, acc_ref, all_ref, columns_ref
):
    blocks, _, lanes = q_ref.shape
    edges = halo_ref.shape[0]
    all_ref[0:blocks] = q_ref[...]
    all_ref[blocks : blocks + edges] = halo_ref[...]

    def clear(b, _):
        acc_ref[b] = jnp.zeros((3, SUB, lanes), f32)
        return 0

    lax.fori_loop(0, blocks + 1, clear, 0)
    turn_columns(halo_ref, columns_ref, edges)

    def one_center(n, _):
        near = [
            (
                index_ref[6 * n + 2 * k],
                index_ref[6 * n + 2 * k + 1],
                step_ref[6 * n + 2 * k],
                step_ref[6 * n + 2 * k + 1],
                False,
            )
            for k in range(3)
        ]
        center_block(all_ref, columns_ref, None, acc_ref, None, n, count_ref[n], near, None)
        return 0

    lax.fori_loop(0, edges, one_center, 0)
    peak_ref[...] = jnp.zeros(peak_ref.shape, f32)

    def close(b, _):
        part = acc_ref[b]
        total = [jnp.sum(part[k], axis=0, keepdims=True) + own_ref[b, k : k + 1, :] for k in range(3)]
        mass = q_ref[b, 6:7, :]
        live = mass > 0.0
        scale = grad_coef / jnp.where(live, mass, 1.0)
        here = pl.ds(b, 1)
        acc_x = jnp.where(live, wind_ref[0, here, :] - scale * total[0], 0.0)
        acc_y = jnp.where(live, wind_ref[1, here, :] - scale * total[1], 0.0)
        out_ref[0, here, :] = acc_x
        out_ref[1, here, :] = acc_y
        out_ref[2, here, :] = jnp.where(live, scale * total[2], 0.0)
        peak_ref[0:1] = jnp.maximum(peak_ref[0:1], acc_x * acc_x + acc_y * acc_y)
        return 0

    lax.fori_loop(0, blocks, close, 0, unroll=4)


def halo_lists(rows, cols):
    index, step = [], []

    def add(r, c, steps):
        for sx, sy in steps:
            inside = 0 <= r + sx < rows and 0 <= c + sy < cols
            block = (r + sx) * cols + c + sy if inside else 0
            index.extend([block, block if inside else rows * cols])
            step.extend([sx, sy])

    for c in range(cols):
        add(-1, c, [(1, -1), (1, 0), (1, 1)])
    for c in range(cols):
        add(rows, c, [(-1, -1), (-1, 0), (-1, 1)])
    for r in range(-1, rows + 1):
        add(r, -1, [(-1, 1), (0, 1), (1, 1)])
    for r in range(-1, rows + 1):
        add(r, cols, [(-1, -1), (0, -1), (1, -1)])
    return np.asarray(index, np.int32), np.asarray(step, np.float32)


def spaces(smem, vmem):
    return [pl.BlockSpec(memory_space=pltpu.SMEM)] * smem + [pl.BlockSpec(memory_space=pltpu.VMEM)] * vmem


def own_forces(counts, positions, velocity, density, mass, rows, cols):
    blocks, lanes = density.shape
    shape = jax.ShapeDtypeStruct((blocks, SUB, lanes), f32)
    return pl.pallas_call(
        functools.partial(own_kernel, rows=rows, cols=cols),
        out_shape=(shape, shape),
        in_specs=spaces(1, 4),
        out_specs=tuple(spaces(0, 2)),
        scratch_shapes=[
            pltpu.VMEM((blocks, 3, SUB, lanes), f32),
            pltpu.VMEM((blocks, lanes, lanes), f32),
            pltpu.VMEM((3, lanes, lanes), f32),
        ],
        compiler_params=pltpu.CompilerParams(vmem_limit_bytes=VMEM_LIMIT),
        cost_estimate=pl.CostEstimate(flops=400_000_000, bytes_accessed=2_000_000, transcendentals=20_000_000),
    )(counts, positions, velocity, density, mass)


def halo_forces(counts, halo, fields, own, wind, rows, cols):
    blocks, _, lanes = fields.shape
    edges = halo.shape[0]
    index, step = halo_lists(rows, cols)
    return pl.pallas_call(
        halo_kernel,
        out_shape=(
            jax.ShapeDtypeStruct((3, blocks, lanes), f32),
            jax.ShapeDtypeStruct((SUB, lanes), f32),
        ),
        in_specs=spaces(3, 4),
        out_specs=tuple(spaces(0, 2)),
        scratch_shapes=[
            pltpu.VMEM((blocks + 1, 3, SUB, lanes), f32),
            pltpu.VMEM((blocks + edges, SUB, lanes), f32),
            pltpu.VMEM((edges, lanes, lanes), f32),
        ],
        compiler_params=pltpu.CompilerParams(vmem_limit_bytes=VMEM_LIMIT),
    )(counts, jnp.asarray(index), jnp.asarray(step), halo, fields, own, wind)


def pick_kernel(slot_ref, keep_ref, table_ref, out_ref):
    count, blocks, lanes = table_ref.shape
    for g in range(slot_ref.shape[0] // SUB):
        here = slice(g * SUB, g * SUB + SUB)
        slots = slot_ref[here]
        block_of = slots // lanes
        lane_of = slots % lanes

        def one(b, picked):
            hit = block_of == b
            rows = [jnp.broadcast_to(table_ref[k, pl.ds(b, 1), :], (SUB, lanes)) for k in range(count)]
            got = [jnp.take_along_axis(row, lane_of, axis=1, mode="promise_in_bounds") for row in rows]
            return tuple(jnp.where(hit, new, old) for new, old in zip(got, picked))

        start = (jnp.zeros((SUB, lanes), f32),) * count
        picked = lax.fori_loop(0, blocks, one, start, unroll=8)
        for k in range(count):
            out_ref[k, here] = picked[k] * keep_ref[here]


def pick(slots, keep, table, ways):
    count = table.shape[0]
    rows, lanes = slots.shape
    picked = pl.pallas_call(
        pick_kernel,
        out_shape=jax.ShapeDtypeStruct((count, rows, lanes), f32),
        in_specs=spaces(0, 3),
        out_specs=pl.BlockSpec(memory_space=pltpu.VMEM),
        compiler_params=pltpu.CompilerParams(vmem_limit_bytes=VMEM_LIMIT),
    )(slots, keep, table)
    return picked.reshape(count, ways, rows // ways, lanes)


def send_on(picked):
    return [
        passed_along(picked[:, 0], "shore", 1),
        passed_along(picked[:, 1], "shore", -1),
        passed_along(picked[:, 2], "cross", 1),
        passed_along(picked[:, 3], "cross", -1),
    ]


def time_step(peak_acc, peak_speed):
    return 0.25 * smooth / (sound_speed + peak_speed + jnp.sqrt(smooth * peak_acc))


def body(
    positions,
    velocity,
    density,
    particle_mass,
    cell_count,
    wind_seed,
    wind_table,
    migrant_slot,
    migrant_count,
):
    _, rows, cols, lanes = positions.shape
    blocks = rows * cols
    slot_ids = jnp.arange(lanes, dtype=jnp.int32)
    alive = slot_ids[None, None, :] < cell_count[:, :, None]
    live = alive.astype(f32)
    live_mass = particle_mass * live
    filled = jnp.broadcast_to(cell_count[:, :, None].astype(f32), live.shape)

    def rows_of(cut):
        there = density[cut]
        parts = [positions[0][cut], positions[1][cut], velocity[0][cut], velocity[1][cut]]
        parts += [there, pressure_ratio(there), live_mass[cut], filled[cut]]
        return jnp.stack(parts, axis=2)

    above = passed_along(rows_of(np.s_[rows - 1 :, :]), "shore", 1)
    below = passed_along(rows_of(np.s_[:1, :]), "shore", -1)
    west = rows_of(np.s_[:, :1])
    east = rows_of(np.s_[:, cols - 1 :])
    left = jnp.concatenate([above[:, cols - 1 :], east, below[:, cols - 1 :]], axis=0)
    right = jnp.concatenate([above[:, :1], west, below[:, :1]], axis=0)
    left, right, held_mass = lax.optimization_barrier((left, right, live_mass))
    left = passed_along(left, "cross", 1)
    right = passed_along(right, "cross", -1)
    halo = jnp.concatenate([z.reshape(-1, SUB, lanes) for z in (above, below, left, right)], axis=0)
    halo_count = halo[:, 7, 0].astype(jnp.int32)

    own, fields = own_forces(
        cell_count.reshape(-1),
        positions.reshape(2, blocks, lanes),
        velocity.reshape(2, blocks, lanes),
        density.reshape(blocks, lanes),
        held_mass.reshape(blocks, lanes),
        rows,
        cols,
    )

    level_ids = jnp.arange(wind_table.shape[1], dtype=jnp.int32)
    one_hot = (wind_seed[None] == level_ids[:, None, None, None]).astype(f32)
    windage = jnp.einsum("cl,lxyp->cxyp", wind_table, one_hot, precision=lax.Precision.HIGHEST)

    ways = migrant_slot.shape[2]
    width = migrant_slot.shape[3]
    slots = migrant_slot.reshape(-1, lanes)
    keep = jnp.arange(width, dtype=jnp.int32)[None, :] < migrant_count.reshape(ways, 1)
    keep = keep.astype(f32).reshape(-1, lanes)
    early = jnp.stack(
        [
            positions[0] * live,
            positions[1] * live,
            velocity[0] * live,
            velocity[1] * live,
            density * live,
            live_mass,
        ]
    )
    came_early = send_on(pick(slots, keep, early.reshape(-1, blocks, lanes), ways))

    late, peak = halo_forces(
        halo_count, halo, fields, own, windage.reshape(2, blocks, lanes), rows, cols
    )
    speed_sq = velocity[0] * velocity[0] + velocity[1] * velocity[1]
    highest = jnp.max(peak, axis=(0, 1), keepdims=True)
    fastest = jnp.max((speed_sq * live).reshape(blocks, lanes), axis=(0, 1), keepdims=True)
    first = lax.broadcasted_iota(jnp.int32, (1, lanes), 1) == 0
    peaks = jnp.sqrt(everywhere_max(jnp.where(first, highest, fastest)))
    delta_t = time_step(peaks[0, 0], peaks[0, 1])
    came_late = send_on(pick(slots, keep, late, ways))

    acceleration = late[:2].reshape(2, rows, cols, lanes)
    rate = late[2].reshape(rows, cols, lanes)
    new_velocity = (velocity + delta_t * acceleration) * live[None]
    new_position = (positions + delta_t * new_velocity) * live[None]
    new_density = (density + delta_t * rate) * live
    state_next = jnp.concatenate([new_position, new_velocity, new_density[None], acceleration])

    at = jnp.stack(came_early)
    on = jnp.stack(came_late)
    moved_velocity = at[:, 2:4] + delta_t * on[:, 0:2]
    moved_position = at[:, 0:2] + delta_t * moved_velocity
    moved_density = at[:, 4:5] + delta_t * on[:, 2:3]
    arrivals = jnp.concatenate(
        [moved_position, moved_velocity, moved_density, at[:, 5:6], on[:, 0:2]], axis=1
    )
    return (state_next, arrivals.reshape(1, 1, ways, arrivals.shape[1], width))


def solution(mesh):
    in_specs = (
        P(None, "shore", "cross", None),
        P(None, "shore", "cross", None),
        P("shore", "cross", None),
        P("shore", "cross", None),
        P("shore", "cross"),
        P("shore", "cross", None),
        P(),
        P("shore", "cross", None, None),
        P("shore", "cross", None),
    )
    out_specs = (P(None, "shore", "cross", None), P("shore", "cross", None, None, None))
    return jax.shard_map(body, mesh=mesh, in_specs=in_specs, out_specs=out_specs, check_vma=False)
```

```python
import functools

import jax
import jax.numpy as jnp
import numpy as np
from jax import lax
from jax.experimental import pallas as pl
from jax.experimental.pallas import tpu as pltpu
from jax.sharding import PartitionSpec as P

sound_speed = 10.0
smooth = 0.5
kernel_norm = 7.0 / (4.0 * 3.141592653589793 * smooth * smooth)
grad_coef = -5.0 * kernel_norm / (smooth * smooth)
f32 = jnp.float32
SUB = 8
GRAN = 2
VMEM_LIMIT = 48 * 1024 * 1024


def passed_along(array, axis, by):
    peers = lax.axis_size(axis)
    pairs = [(i, i + by) for i in range(peers) if 0 <= i + by < peers]
    return lax.ppermute(array, axis, pairs)


def everywhere_max(array):
    for axis in ("cross", "shore"):
        peers = lax.axis_size(axis)
        step = 1
        while step < peers:
            if peers & (peers - 1) == 0:
                pairs = [(i, i ^ step) for i in range(peers)]
            else:
                pairs = [(i, (i + step) % peers) for i in range(peers)]
            array = jnp.maximum(array, lax.ppermute(array, axis, pairs))
            step *= 2
    return array


def pressure_ratio(density):
    cube = density * density * density
    seventh = cube * cube * density
    pressure = sound_speed * sound_speed / 7.0 * (seventh - 1.0)
    return pressure / (density * density)


def pair_terms(own, near):
    dx = own[0] - near[0]
    dy = own[1] - near[1]
    dist_sq = dx * dx + dy * dy
    guarded = jnp.maximum(dist_sq, 1e-30)
    radius = guarded * lax.rsqrt(guarded)
    falloff = jnp.maximum(1.0 - radius, 0.0)
    weight = (falloff * falloff) * (falloff * (own[6] * near[6]))
    approach = (own[2] - near[2]) * dx + (own[3] - near[3]) * dy
    bottom = (dist_sq + 0.01 * smooth * smooth) * (own[4] + near[4])
    total = (own[5] + near[5]) - jnp.minimum(approach, 0.0) * pltpu.reciprocal(bottom, approx=True)
    shared = weight * total
    return shared * dx, shared * dy, weight * approach


def plus(total, term):
    return term if total is None else tuple(a + b for a, b in zip(total, term))


def center_tiles(q_ref, columns_ref, behind_ref, acc_ref, rows_ref, center, tiles, near, before):
    lanes = q_ref.shape[2]
    if before is not None:
        close_behind(behind_ref, rows_ref, before)
    others = []
    for block, _, step_x, step_y, _ in near:
        fields = [q_ref[block, k : k + 1, :] for k in range(7)]
        fields[0] = fields[0] + step_x
        fields[1] = fields[1] + step_y
        others.append([jnp.broadcast_to(f, (SUB, lanes)) for f in fields])
    sums = [None] * len(near)
    for t in range(tiles):
        tile = columns_ref[center, SUB * t : SUB * t + SUB, 0:SUB]
        mine = [jnp.broadcast_to(tile[:, k : k + 1], (SUB, lanes)) for k in range(7)]
        behind = None
        for n in range(len(near)):
            term = pair_terms(others[n], mine)
            sums[n] = plus(sums[n], term)
            if near[n][4]:
                behind = plus(behind, term)
        if behind is not None:
            for k in range(3):
                behind_ref[k, SUB * t : SUB * t + SUB, :] = behind[k]
    for n in range(len(near)):
        for k in range(3):
            acc_ref[near[n][1], k] = acc_ref[near[n][1], k] + sums[n][k]


def close_behind(behind_ref, rows_ref, center):
    lanes = behind_ref.shape[2]
    ones = jnp.ones((16, lanes), jnp.bfloat16)
    dims = (((1,), (1,)), ((), ()))
    sub = lax.broadcasted_iota(jnp.int32, (SUB, lanes), 0)
    total = jnp.zeros((SUB, lanes), f32)
    for k in range(3):
        part = behind_ref[k]
        high = part.astype(jnp.bfloat16)
        low = (part - high.astype(f32)).astype(jnp.bfloat16)
        row = sum(
            lax.dot_general(ones, piece, dims, preferred_element_type=f32) for piece in (high, low)
        )
        total = jnp.where(sub == k, row[:SUB], total)
    rows_ref[center] = total


def center_block(q_ref, columns_ref, behind_ref, acc_ref, rows_ref, center, count, near, before):
    most = q_ref.shape[2] // SUB
    tiles = pl.cdiv(count, SUB * GRAN)
    for v in range(0 if before is not None else 1, most // GRAN + 1):

        @pl.when(tiles == v)
        def _():
            if v == 0:
                close_behind(behind_ref, rows_ref, before)
                behind_ref[...] = jnp.zeros(behind_ref.shape, f32)
            else:
                center_tiles(
                    q_ref, columns_ref, behind_ref, acc_ref, rows_ref, center, v * GRAN, near, before
                )


def turn_columns(q_ref, columns_ref, blocks):
    def turn(b, _):
        columns_ref[b, :, 0:SUB] = jnp.transpose(q_ref[b])
        return 0

    lax.fori_loop(0, blocks, turn, 0, unroll=4)


def own_kernel(
    count_ref, pos_ref, vel_ref, rho_ref, mass_ref, out_ref, q_ref, acc_ref, columns_ref, behind_ref, *, rows, cols
):
    blocks = rows * cols
    lanes = q_ref.shape[2]
    flat = q_ref.reshape(blocks * SUB, lanes)

    def fill(g, _):
        here = pl.ds(pl.multiple_of(g * SUB, SUB), SUB)
        density = rho_ref[here, :]
        values = [
            pos_ref[0, here, :],
            pos_ref[1, here, :],
            vel_ref[0, here, :],
            vel_ref[1, here, :],
            density,
            pressure_ratio(density),
            mass_ref[here, :],
            density,
        ]
        for k in range(SUB):
            flat[pl.ds(g * SUB * SUB + k, SUB, stride=SUB), :] = values[k]
        return 0

    lax.fori_loop(0, blocks // SUB, fill, 0)

    def clear(b, _):
        acc_ref[b] = jnp.zeros((3, SUB, lanes), f32)
        return 0

    lax.fori_loop(0, blocks, clear, 0, unroll=4)
    behind_ref[...] = jnp.zeros(behind_ref.shape, f32)
    turn_columns(q_ref, columns_ref, blocks)

    def run(r, c, steps):
        center = r * cols + c
        near = [
            (center + sx * cols + sy, center + sx * cols + sy, float(sx), float(sy), (sx, sy) != (0, 0))
            for sx, sy in steps
        ]
        center_block(
            q_ref, columns_ref, behind_ref, acc_ref, out_ref, center, count_ref[center], near,
            jnp.maximum(center - 1, 0),
        )

    def one_row(r, _):
        run(r, 0, [(0, 1), (1, 0), (1, 1), (0, 0)])

        def middle(c, _):
            run(r, c, [(0, 1), (1, -1), (1, 0), (1, 1), (0, 0)])
            return 0

        lax.fori_loop(1, cols - 1, middle, 0)
        run(r, cols - 1, [(1, -1), (1, 0), (0, 0)])
        return 0

    lax.fori_loop(0, rows - 1, one_row, 0)

    def last_row(c, _):
        run(rows - 1, c, [(0, 1), (0, 0)])
        return 0

    lax.fori_loop(0, cols - 1, last_row, 0)
    run(rows - 1, cols - 1, [(0, 0)])
    out_ref[blocks - 1] = jnp.zeros((SUB, lanes), f32)
    sub = lax.broadcasted_iota(jnp.int32, (SUB, lanes), 0)

    def close(b, _):
        part = acc_ref[b]
        rows_sum = [jnp.sum(part[k], axis=0, keepdims=True) for k in range(3)]
        front = jnp.concatenate(rows_sum + [jnp.zeros((SUB - 3, lanes), f32)], axis=0)
        behind = out_ref[b]
        out_ref[b] = jnp.where(sub == 2, front + behind, front - behind)
        return 0

    lax.fori_loop(0, blocks, close, 0, unroll=4)


def halo_kernel(
    count_ref, index_ref, step_ref, halo_ref, q_ref, own_ref, wind_ref, out_ref, peak_ref, acc_ref, all_ref, columns_ref
):
    blocks, _, lanes = q_ref.shape
    edges = halo_ref.shape[0]
    all_ref[0:blocks] = q_ref[...]
    all_ref[blocks : blocks + edges] = halo_ref[...]

    def clear(b, _):
        acc_ref[b] = jnp.zeros((3, SUB, lanes), f32)
        return 0

    lax.fori_loop(0, blocks + 1, clear, 0)
    turn_columns(halo_ref, columns_ref, edges)

    def one_center(n, _):
        near = [
            (
                index_ref[6 * n + 2 * k],
                index_ref[6 * n + 2 * k + 1],
                step_ref[6 * n + 2 * k],
                step_ref[6 * n + 2 * k + 1],
                False,
            )
            for k in range(3)
        ]
        center_block(all_ref, columns_ref, None, acc_ref, None, n, count_ref[n], near, None)
        return 0

    lax.fori_loop(0, edges, one_center, 0)
    nothing = jnp.zeros((1, lanes), f32)

    def close(b, peaks):
        part = acc_ref[b]
        total = [jnp.sum(part[k], axis=0, keepdims=True) + own_ref[b, k : k + 1, :] for k in range(3)]
        speed_x, speed_y, mass = (q_ref[b, k : k + 1, :] for k in (2, 3, 6))
        live = mass > 0.0
        scale = grad_coef / jnp.where(live, mass, 1.0)
        here = pl.ds(b, 1)
        acc_x = jnp.where(live, wind_ref[0, here, :] - scale * total[0], 0.0)
        acc_y = jnp.where(live, wind_ref[1, here, :] - scale * total[1], 0.0)
        out_ref[0, here, :] = acc_x
        out_ref[1, here, :] = acc_y
        out_ref[2, here, :] = jnp.where(live, scale * total[2], 0.0)
        speed = jnp.where(live, speed_x * speed_x + speed_y * speed_y, 0.0)
        return jnp.maximum(peaks[0], acc_x * acc_x + acc_y * acc_y), jnp.maximum(peaks[1], speed)

    highest, fastest = lax.fori_loop(0, blocks, close, (nothing, nothing), unroll=4)
    highest = jnp.max(highest, axis=1, keepdims=True)
    fastest = jnp.max(fastest, axis=1, keepdims=True)
    first = lax.broadcasted_iota(jnp.int32, peak_ref.shape, 1) == 0
    peak_ref[...] = jnp.where(first, highest, fastest)


def halo_lists(rows, cols):
    index, step = [], []

    def add(r, c, steps):
        for sx, sy in steps:
            inside = 0 <= r + sx < rows and 0 <= c + sy < cols
            block = (r + sx) * cols + c + sy if inside else 0
            index.extend([block, block if inside else rows * cols])
            step.extend([sx, sy])

    for c in range(cols):
        add(-1, c, [(1, -1), (1, 0), (1, 1)])
    for c in range(cols):
        add(rows, c, [(-1, -1), (-1, 0), (-1, 1)])
    for r in range(-1, rows + 1):
        add(r, -1, [(-1, 1), (0, 1), (1, 1)])
    for r in range(-1, rows + 1):
        add(r, cols, [(-1, -1), (0, -1), (1, -1)])
    return np.asarray(index, np.int32), np.asarray(step, np.float32)


def spaces(smem, vmem):
    return [pl.BlockSpec(memory_space=pltpu.SMEM)] * smem + [pl.BlockSpec(memory_space=pltpu.VMEM)] * vmem


def own_forces(counts, positions, velocity, density, mass, rows, cols):
    blocks, lanes = density.shape
    shape = jax.ShapeDtypeStruct((blocks, SUB, lanes), f32)
    return pl.pallas_call(
        functools.partial(own_kernel, rows=rows, cols=cols),
        out_shape=(shape, shape),
        in_specs=spaces(1, 4),
        out_specs=tuple(spaces(0, 2)),
        scratch_shapes=[
            pltpu.VMEM((blocks, 3, SUB, lanes), f32),
            pltpu.VMEM((blocks, lanes, lanes), f32),
            pltpu.VMEM((3, lanes, lanes), f32),
        ],
        compiler_params=pltpu.CompilerParams(vmem_limit_bytes=VMEM_LIMIT),
        cost_estimate=pl.CostEstimate(flops=400_000_000, bytes_accessed=2_000_000, transcendentals=20_000_000),
    )(counts, positions, velocity, density, mass)


def halo_forces(counts, halo, fields, own, wind, rows, cols):
    blocks, _, lanes = fields.shape
    edges = halo.shape[0]
    index, step = halo_lists(rows, cols)
    return pl.pallas_call(
        halo_kernel,
        out_shape=(
            jax.ShapeDtypeStruct((3, blocks, lanes), f32),
            jax.ShapeDtypeStruct((SUB, lanes), f32),
        ),
        in_specs=spaces(3, 4),
        out_specs=tuple(spaces(0, 2)),
        scratch_shapes=[
            pltpu.VMEM((blocks + 1, 3, SUB, lanes), f32),
            pltpu.VMEM((blocks + edges, SUB, lanes), f32),
            pltpu.VMEM((edges, lanes, lanes), f32),
        ],
        compiler_params=pltpu.CompilerParams(vmem_limit_bytes=VMEM_LIMIT),
    )(counts, jnp.asarray(index), jnp.asarray(step), halo, fields, own, wind)


def pick_kernel(slot_ref, keep_ref, table_ref, out_ref):
    count, blocks, lanes = table_ref.shape
    sub = lax.broadcasted_iota(jnp.int32, (SUB, lanes), 0)

    def group(g, _):
        here = pl.ds(pl.multiple_of(g * SUB, SUB), SUB)
        slots = slot_ref[here, :]
        keep = keep_ref[here, :]
        outs = [jnp.zeros((SUB, lanes), f32)] * count
        for r in range(SUB):
            wanted = jnp.broadcast_to(slots[r : r + 1], (SUB, lanes))
            lane_of = wanted % lanes
            offset = wanted // lanes - sub
            picked = [jnp.zeros((SUB, lanes), f32)] * count
            for t in range(0, blocks, SUB):
                hit = offset == t
                for k in range(count):
                    got = jnp.take_along_axis(
                        table_ref[k, t : t + SUB, :], lane_of, axis=1, mode="promise_in_bounds"
                    )
                    picked[k] = jnp.where(hit, got, picked[k])
            for k in range(count):
                outs[k] = jnp.where(sub == r, jnp.sum(picked[k], axis=0, keepdims=True), outs[k])
        for k in range(count):
            out_ref[k, here, :] = outs[k] * keep
        return 0

    lax.fori_loop(0, slot_ref.shape[0] // SUB, group, 0)


def pick(slots, keep, table, ways):
    count = table.shape[0]
    rows, lanes = slots.shape
    picked = pl.pallas_call(
        pick_kernel,
        out_shape=jax.ShapeDtypeStruct((count, rows, lanes), f32),
        in_specs=spaces(0, 3),
        out_specs=pl.BlockSpec(memory_space=pltpu.VMEM),
        compiler_params=pltpu.CompilerParams(vmem_limit_bytes=VMEM_LIMIT),
    )(slots, keep, table)
    return picked.reshape(count, ways, rows // ways, lanes)


def send_on(picked):
    return [
        passed_along(picked[:, 0], "shore", 1),
        passed_along(picked[:, 1], "shore", -1),
        passed_along(picked[:, 2], "cross", 1),
        passed_along(picked[:, 3], "cross", -1),
    ]


def time_step(peak_acc, peak_speed):
    return 0.25 * smooth / (sound_speed + peak_speed + jnp.sqrt(smooth * peak_acc))


def body(
    positions,
    velocity,
    density,
    particle_mass,
    cell_count,
    wind_seed,
    wind_table,
    migrant_slot,
    migrant_count,
):
    _, rows, cols, lanes = positions.shape
    blocks = rows * cols
    slot_ids = jnp.arange(lanes, dtype=jnp.int32)
    alive = slot_ids[None, None, :] < cell_count[:, :, None]
    live = alive.astype(f32)
    live_mass = particle_mass * live
    filled = jnp.broadcast_to(cell_count[:, :, None].astype(f32), live.shape)

    def rows_of(cut):
        there = density[cut]
        parts = [positions[0][cut], positions[1][cut], velocity[0][cut], velocity[1][cut]]
        parts += [there, pressure_ratio(there), live_mass[cut], filled[cut]]
        return jnp.stack(parts, axis=2)

    above = passed_along(rows_of(np.s_[rows - 1 :, :]), "shore", 1)
    below = passed_along(rows_of(np.s_[:1, :]), "shore", -1)
    west = rows_of(np.s_[:, :1])
    east = rows_of(np.s_[:, cols - 1 :])
    left = jnp.concatenate([above[:, cols - 1 :], east, below[:, cols - 1 :]], axis=0)
    right = jnp.concatenate([above[:, :1], west, below[:, :1]], axis=0)
    left, right, held_mass = lax.optimization_barrier((left, right, live_mass))
    left = passed_along(left, "cross", 1)
    right = passed_along(right, "cross", -1)
    halo = jnp.concatenate([z.reshape(-1, SUB, lanes) for z in (above, below, left, right)], axis=0)
    halo_count = halo[:, 7, 0].astype(jnp.int32)

    own, fields = own_forces(
        cell_count.reshape(-1),
        positions.reshape(2, blocks, lanes),
        velocity.reshape(2, blocks, lanes),
        density.reshape(blocks, lanes),
        held_mass.reshape(blocks, lanes),
        rows,
        cols,
    )

    level_ids = jnp.arange(wind_table.shape[1], dtype=jnp.int32)
    one_hot = (wind_seed[None] == level_ids[:, None, None, None]).astype(f32)
    windage = jnp.einsum("cl,lxyp->cxyp", wind_table, one_hot, precision=lax.Precision.HIGHEST)

    ways = migrant_slot.shape[2]
    width = migrant_slot.shape[3]
    slots = migrant_slot.reshape(-1, lanes)
    keep = jnp.arange(width, dtype=jnp.int32)[None, :] < migrant_count.reshape(ways, 1)
    keep = keep.astype(f32).reshape(-1, lanes)
    early = jnp.stack(
        [
            positions[0] * live,
            positions[1] * live,
            velocity[0] * live,
            velocity[1] * live,
            density * live,
            live_mass,
        ]
    )
    still = pick(slots, keep, early.reshape(-1, blocks, lanes), ways)

    late, peak = halo_forces(
        halo_count, halo, fields, own, windage.reshape(2, blocks, lanes), rows, cols
    )
    peaks = jnp.sqrt(everywhere_max(peak))
    delta_t = time_step(peaks[0, 0], peaks[0, 1])
    moving = pick(slots, keep, late, ways)
    came = jnp.stack(send_on(jnp.concatenate([still, moving])))

    acceleration = late[:2].reshape(2, rows, cols, lanes)
    rate = late[2].reshape(rows, cols, lanes)
    new_velocity = (velocity + delta_t * acceleration) * live[None]
    new_position = (positions + delta_t * new_velocity) * live[None]
    new_density = (density + delta_t * rate) * live
    state_next = jnp.concatenate([new_position, new_velocity, new_density[None], acceleration])

    moved_velocity = came[:, 2:4] + delta_t * came[:, 6:8]
    moved_position = came[:, 0:2] + delta_t * moved_velocity
    moved_density = came[:, 4:5] + delta_t * came[:, 8:9]
    arrivals = jnp.concatenate(
        [moved_position, moved_velocity, moved_density, came[:, 5:6], came[:, 6:8]], axis=1
    )
    return (state_next, arrivals.reshape(1, 1, ways, arrivals.shape[1], width))


def solution(mesh):
    in_specs = (
        P(None, "shore", "cross", None),
        P(None, "shore", "cross", None),
        P("shore", "cross", None),
        P("shore", "cross", None),
        P("shore", "cross"),
        P("shore", "cross", None),
        P(),
        P("shore", "cross", None, None),
        P("shore", "cross", None),
    )
    out_specs = (P(None, "shore", "cross", None), P("shore", "cross", None, None, None))
    return jax.shard_map(body, mesh=mesh, in_specs=in_specs, out_specs=out_specs, check_vma=False)
```

```python
import functools

import jax
import jax.numpy as jnp
import numpy as np
from jax import lax
from jax.experimental import pallas as pl
from jax.experimental.pallas import tpu as pltpu
from jax.sharding import PartitionSpec as P

sound_speed = 10.0
smooth = 0.5
kernel_norm = 7.0 / (4.0 * 3.141592653589793 * smooth * smooth)
grad_coef = -5.0 * kernel_norm / (smooth * smooth)
f32 = jnp.float32
SUB = 8
GRAN = 2
VMEM_LIMIT = 48 * 1024 * 1024


def passed_along(array, axis, by):
    peers = lax.axis_size(axis)
    pairs = [(i, i + by) for i in range(peers) if 0 <= i + by < peers]
    return lax.ppermute(array, axis, pairs)


def everywhere_max(array):
    for axis in ("cross", "shore"):
        peers = lax.axis_size(axis)
        step = 1
        while step < peers:
            if peers & (peers - 1) == 0:
                pairs = [(i, i ^ step) for i in range(peers)]
            else:
                pairs = [(i, (i + step) % peers) for i in range(peers)]
            array = jnp.maximum(array, lax.ppermute(array, axis, pairs))
            step *= 2
    return array


def pressure_ratio(density):
    cube = density * density * density
    seventh = cube * cube * density
    pressure = sound_speed * sound_speed / 7.0 * (seventh - 1.0)
    return pressure / (density * density)


def pair_terms(own, near):
    dx = own[0] - near[0]
    dy = own[1] - near[1]
    dist_sq = dx * dx + dy * dy
    guarded = jnp.maximum(dist_sq, 1e-30)
    radius = guarded * lax.rsqrt(guarded)
    falloff = jnp.maximum(1.0 - radius, 0.0)
    weight = (falloff * falloff) * (falloff * (own[6] * near[6]))
    approach = (own[2] - near[2]) * dx + (own[3] - near[3]) * dy
    bottom = (dist_sq + 0.01 * smooth * smooth) * (own[4] + near[4])
    total = (own[5] + near[5]) - jnp.minimum(approach, 0.0) * pltpu.reciprocal(bottom, approx=True)
    shared = weight * total
    return shared * dx, shared * dy, weight * approach


def plus(total, term):
    return term if total is None else tuple(a + b for a, b in zip(total, term))


def center_tiles(q_ref, columns_ref, behind_ref, acc_ref, rows_ref, center, tiles, near, before):
    lanes = q_ref.shape[2]
    if before is not None:
        close_behind(behind_ref, rows_ref, before)
    others = []
    for block, _, step_x, step_y, _ in near:
        fields = [q_ref[block, k : k + 1, :] for k in range(7)]
        fields[0] = fields[0] + step_x
        fields[1] = fields[1] + step_y
        others.append([jnp.broadcast_to(f, (SUB, lanes)) for f in fields])
    sums = [None] * len(near)
    for t in range(tiles):
        tile = columns_ref[center, SUB * t : SUB * t + SUB, 0:SUB]
        mine = [jnp.broadcast_to(tile[:, k : k + 1], (SUB, lanes)) for k in range(7)]
        behind = None
        for n in range(len(near)):
            term = pair_terms(others[n], mine)
            sums[n] = plus(sums[n], term)
            if near[n][4]:
                behind = plus(behind, term)
        if behind is not None:
            for k in range(3):
                behind_ref[k, SUB * t : SUB * t + SUB, :] = behind[k]
    for n in range(len(near)):
        for k in range(3):
            acc_ref[near[n][1], k] = acc_ref[near[n][1], k] + sums[n][k]


def close_behind(behind_ref, rows_ref, center):
    lanes = behind_ref.shape[2]
    ones = jnp.ones((16, lanes), jnp.bfloat16)
    dims = (((1,), (1,)), ((), ()))
    sub = lax.broadcasted_iota(jnp.int32, (SUB, lanes), 0)
    total = jnp.zeros((SUB, lanes), f32)
    for k in range(3):
        part = behind_ref[k]
        high = part.astype(jnp.bfloat16)
        low = (part - high.astype(f32)).astype(jnp.bfloat16)
        row = sum(
            lax.dot_general(ones, piece, dims, preferred_element_type=f32) for piece in (high, low)
        )
        total = jnp.where(sub == k, row[:SUB], total)
    rows_ref[center] = total


def center_block(q_ref, columns_ref, behind_ref, acc_ref, rows_ref, center, count, near, before):
    most = q_ref.shape[2] // SUB
    tiles = pl.cdiv(count, SUB * GRAN)
    for v in range(0 if before is not None else 1, most // GRAN + 1):

        @pl.when(tiles == v)
        def _():
            if v == 0:
                close_behind(behind_ref, rows_ref, before)
                behind_ref[...] = jnp.zeros(behind_ref.shape, f32)
            else:
                center_tiles(
                    q_ref, columns_ref, behind_ref, acc_ref, rows_ref, center, v * GRAN, near, before
                )


def turn_columns(q_ref, columns_ref, blocks):
    lanes = q_ref.shape[2]
    most = lanes // SUB
    at_once = max(n for n in range(1, most + 1) if blocks % n == 0)

    def turn(g, _):
        rows = [q_ref[g * at_once + n] for n in range(at_once)]
        rows += [jnp.zeros((SUB, lanes), f32)] * (most - at_once)
        turned = jnp.transpose(jnp.concatenate(rows, axis=0))
        for n in range(at_once):
            columns_ref[g * at_once + n, :, 0:SUB] = turned[:, n * SUB : n * SUB + SUB]
        return 0

    lax.fori_loop(0, blocks // at_once, turn, 0)


def own_kernel(
    count_ref, pos_ref, vel_ref, rho_ref, mass_ref, out_ref, q_ref, acc_ref, columns_ref, behind_ref, *, rows, cols
):
    blocks = rows * cols
    lanes = q_ref.shape[2]
    flat = q_ref.reshape(blocks * SUB, lanes)

    def fill(g, _):
        here = pl.ds(pl.multiple_of(g * SUB, SUB), SUB)
        density = rho_ref[here, :]
        values = [
            pos_ref[0, here, :],
            pos_ref[1, here, :],
            vel_ref[0, here, :],
            vel_ref[1, here, :],
            density,
            pressure_ratio(density),
            mass_ref[here, :],
            density,
        ]
        for k in range(SUB):
            flat[pl.ds(g * SUB * SUB + k, SUB, stride=SUB), :] = values[k]
        return 0

    lax.fori_loop(0, blocks // SUB, fill, 0)

    def clear(b, _):
        acc_ref[b] = jnp.zeros((3, SUB, lanes), f32)
        return 0

    lax.fori_loop(0, blocks, clear, 0, unroll=4)
    behind_ref[...] = jnp.zeros(behind_ref.shape, f32)
    turn_columns(q_ref, columns_ref, blocks)

    def run(r, c, steps):
        center = r * cols + c
        near = [
            (center + sx * cols + sy, center + sx * cols + sy, float(sx), float(sy), (sx, sy) != (0, 0))
            for sx, sy in steps
        ]
        center_block(
            q_ref, columns_ref, behind_ref, acc_ref, out_ref, center, count_ref[center], near,
            jnp.maximum(center - 1, 0),
        )

    def one_row(r, _):
        run(r, 0, [(0, 1), (1, 0), (1, 1), (0, 0)])

        def middle(c, _):
            run(r, c, [(0, 1), (1, -1), (1, 0), (1, 1), (0, 0)])
            return 0

        lax.fori_loop(1, cols - 1, middle, 0)
        run(r, cols - 1, [(1, -1), (1, 0), (0, 0)])
        return 0

    lax.fori_loop(0, rows - 1, one_row, 0)

    def last_row(c, _):
        run(rows - 1, c, [(0, 1), (0, 0)])
        return 0

    lax.fori_loop(0, cols - 1, last_row, 0)
    run(rows - 1, cols - 1, [(0, 0)])
    out_ref[blocks - 1] = jnp.zeros((SUB, lanes), f32)
    sub = lax.broadcasted_iota(jnp.int32, (SUB, lanes), 0)

    def close(b, _):
        part = acc_ref[b]
        rows_sum = [jnp.sum(part[k], axis=0, keepdims=True) for k in range(3)]
        front = jnp.concatenate(rows_sum + [jnp.zeros((SUB - 3, lanes), f32)], axis=0)
        behind = out_ref[b]
        out_ref[b] = jnp.where(sub == 2, front + behind, front - behind)
        return 0

    lax.fori_loop(0, blocks, close, 0, unroll=4)


def halo_kernel(
    count_ref, index_ref, step_ref, halo_ref, q_ref, own_ref, wind_ref, out_ref, peak_ref, acc_ref, all_ref, columns_ref
):
    blocks, _, lanes = q_ref.shape
    edges = halo_ref.shape[0]
    all_ref[0:blocks] = q_ref[...]
    all_ref[blocks : blocks + edges] = halo_ref[...]

    def clear(b, _):
        acc_ref[b] = jnp.zeros((3, SUB, lanes), f32)
        return 0

    lax.fori_loop(0, blocks + 1, clear, 0)
    turn_columns(halo_ref, columns_ref, edges)

    def one_center(n, _):
        near = [
            (
                index_ref[6 * n + 2 * k],
                index_ref[6 * n + 2 * k + 1],
                step_ref[6 * n + 2 * k],
                step_ref[6 * n + 2 * k + 1],
                False,
            )
            for k in range(3)
        ]
        center_block(all_ref, columns_ref, None, acc_ref, None, n, count_ref[n], near, None)
        return 0

    lax.fori_loop(0, edges, one_center, 0)
    nothing = jnp.zeros((1, lanes), f32)

    def close(b, peaks):
        part = acc_ref[b]
        total = [jnp.sum(part[k], axis=0, keepdims=True) + own_ref[b, k : k + 1, :] for k in range(3)]
        speed_x, speed_y, mass = (q_ref[b, k : k + 1, :] for k in (2, 3, 6))
        live = mass > 0.0
        scale = grad_coef / jnp.where(live, mass, 1.0)
        here = pl.ds(b, 1)
        acc_x = jnp.where(live, wind_ref[0, here, :] - scale * total[0], 0.0)
        acc_y = jnp.where(live, wind_ref[1, here, :] - scale * total[1], 0.0)
        out_ref[0, here, :] = acc_x
        out_ref[1, here, :] = acc_y
        out_ref[2, here, :] = jnp.where(live, scale * total[2], 0.0)
        speed = jnp.where(live, speed_x * speed_x + speed_y * speed_y, 0.0)
        return jnp.maximum(peaks[0], acc_x * acc_x + acc_y * acc_y), jnp.maximum(peaks[1], speed)

    highest, fastest = lax.fori_loop(0, blocks, close, (nothing, nothing), unroll=4)
    highest = jnp.max(highest, axis=1, keepdims=True)
    fastest = jnp.max(fastest, axis=1, keepdims=True)
    first = lax.broadcasted_iota(jnp.int32, peak_ref.shape, 0) == 0
    peak_ref[...] = jnp.where(first, highest, fastest)


def halo_lists(rows, cols):
    index, step = [], []

    def add(r, c, steps):
        for sx, sy in steps:
            inside = 0 <= r + sx < rows and 0 <= c + sy < cols
            block = (r + sx) * cols + c + sy if inside else 0
            index.extend([block, block if inside else rows * cols])
            step.extend([sx, sy])

    for c in range(cols):
        add(-1, c, [(1, -1), (1, 0), (1, 1)])
    for c in range(cols):
        add(rows, c, [(-1, -1), (-1, 0), (-1, 1)])
    for r in range(-1, rows + 1):
        add(r, -1, [(-1, 1), (0, 1), (1, 1)])
    for r in range(-1, rows + 1):
        add(r, cols, [(-1, -1), (0, -1), (1, -1)])
    return np.asarray(index, np.int32), np.asarray(step, np.float32)


def spaces(smem, vmem):
    return [pl.BlockSpec(memory_space=pltpu.SMEM)] * smem + [pl.BlockSpec(memory_space=pltpu.VMEM)] * vmem


def own_forces(counts, positions, velocity, density, mass, rows, cols):
    blocks, lanes = density.shape
    shape = jax.ShapeDtypeStruct((blocks, SUB, lanes), f32)
    return pl.pallas_call(
        functools.partial(own_kernel, rows=rows, cols=cols),
        out_shape=(shape, shape),
        in_specs=spaces(1, 4),
        out_specs=tuple(spaces(0, 2)),
        scratch_shapes=[
            pltpu.VMEM((blocks, 3, SUB, lanes), f32),
            pltpu.VMEM((blocks, lanes, lanes), f32),
            pltpu.VMEM((3, lanes, lanes), f32),
        ],
        compiler_params=pltpu.CompilerParams(vmem_limit_bytes=VMEM_LIMIT),
        cost_estimate=pl.CostEstimate(flops=400_000_000, bytes_accessed=2_000_000, transcendentals=20_000_000),
    )(counts, positions, velocity, density, mass)


def halo_forces(counts, halo, fields, own, wind, rows, cols):
    blocks, _, lanes = fields.shape
    edges = halo.shape[0]
    index, step = halo_lists(rows, cols)
    return pl.pallas_call(
        halo_kernel,
        out_shape=(
            jax.ShapeDtypeStruct((3, blocks, lanes), f32),
            jax.ShapeDtypeStruct((SUB, lanes), f32),
        ),
        in_specs=spaces(3, 4),
        out_specs=tuple(spaces(0, 2)),
        scratch_shapes=[
            pltpu.VMEM((blocks + 1, 3, SUB, lanes), f32),
            pltpu.VMEM((blocks + edges, SUB, lanes), f32),
            pltpu.VMEM((edges, lanes, lanes), f32),
        ],
        compiler_params=pltpu.CompilerParams(vmem_limit_bytes=VMEM_LIMIT),
    )(counts, jnp.asarray(index), jnp.asarray(step), halo, fields, own, wind)


def pick_kernel(slot_ref, keep_ref, table_ref, out_ref):
    count, blocks, lanes = table_ref.shape
    sub = lax.broadcasted_iota(jnp.int32, (SUB, lanes), 0)

    def group(g, _):
        here = pl.ds(pl.multiple_of(g * SUB, SUB), SUB)
        slots = slot_ref[here, :]
        keep = keep_ref[here, :]
        outs = [jnp.zeros((SUB, lanes), f32)] * count
        for r in range(SUB):
            wanted = jnp.broadcast_to(slots[r : r + 1], (SUB, lanes))
            lane_of = wanted % lanes
            offset = wanted // lanes - sub
            picked = [jnp.zeros((SUB, lanes), f32)] * count
            for t in range(0, blocks, SUB):
                hit = offset == t
                for k in range(count):
                    got = jnp.take_along_axis(
                        table_ref[k, t : t + SUB, :], lane_of, axis=1, mode="promise_in_bounds"
                    )
                    picked[k] = jnp.where(hit, got, picked[k])
            for k in range(count):
                outs[k] = jnp.where(sub == r, jnp.sum(picked[k], axis=0, keepdims=True), outs[k])
        for k in range(count):
            out_ref[k, here, :] = outs[k] * keep
        return 0

    lax.fori_loop(0, slot_ref.shape[0] // SUB, group, 0)


def pick(slots, keep, table, ways):
    count = table.shape[0]
    rows, lanes = slots.shape
    picked = pl.pallas_call(
        pick_kernel,
        out_shape=jax.ShapeDtypeStruct((count, rows, lanes), f32),
        in_specs=spaces(0, 3),
        out_specs=pl.BlockSpec(memory_space=pltpu.VMEM),
        compiler_params=pltpu.CompilerParams(vmem_limit_bytes=VMEM_LIMIT),
    )(slots, keep, table)
    return picked.reshape(count, ways, rows // ways, lanes)


def send_on(picked):
    return [
        passed_along(picked[:, 0], "shore", 1),
        passed_along(picked[:, 1], "shore", -1),
        passed_along(picked[:, 2], "cross", 1),
        passed_along(picked[:, 3], "cross", -1),
    ]


def time_step(peak_acc, peak_speed):
    return 0.25 * smooth / (sound_speed + peak_speed + jnp.sqrt(smooth * peak_acc))


def body(
    positions,
    velocity,
    density,
    particle_mass,
    cell_count,
    wind_seed,
    wind_table,
    migrant_slot,
    migrant_count,
):
    _, rows, cols, lanes = positions.shape
    blocks = rows * cols
    slot_ids = jnp.arange(lanes, dtype=jnp.int32)
    alive = slot_ids[None, None, :] < cell_count[:, :, None]
    live = alive.astype(f32)
    live_mass = particle_mass * live
    filled = jnp.broadcast_to(cell_count[:, :, None].astype(f32), live.shape)

    def rows_of(cut):
        there = density[cut]
        parts = [positions[0][cut], positions[1][cut], velocity[0][cut], velocity[1][cut]]
        parts += [there, pressure_ratio(there), live_mass[cut], filled[cut]]
        return jnp.stack(parts, axis=2)

    above = passed_along(rows_of(np.s_[rows - 1 :, :]), "shore", 1)
    below = passed_along(rows_of(np.s_[:1, :]), "shore", -1)
    west = rows_of(np.s_[:, :1])
    east = rows_of(np.s_[:, cols - 1 :])
    left = jnp.concatenate([above[:, cols - 1 :], east, below[:, cols - 1 :]], axis=0)
    right = jnp.concatenate([above[:, :1], west, below[:, :1]], axis=0)
    left, right, held_mass = lax.optimization_barrier((left, right, live_mass))
    left = passed_along(left, "cross", 1)
    right = passed_along(right, "cross", -1)
    halo = jnp.concatenate([z.reshape(-1, SUB, lanes) for z in (above, below, left, right)], axis=0)
    halo_count = halo[:, 7, 0].astype(jnp.int32)

    own, fields = own_forces(
        cell_count.reshape(-1),
        positions.reshape(2, blocks, lanes),
        velocity.reshape(2, blocks, lanes),
        density.reshape(blocks, lanes),
        held_mass.reshape(blocks, lanes),
        rows,
        cols,
    )

    level_ids = jnp.arange(wind_table.shape[1], dtype=jnp.int32)
    one_hot = (wind_seed[None] == level_ids[:, None, None, None]).astype(f32)
    windage = jnp.einsum("cl,lxyp->cxyp", wind_table, one_hot, precision=lax.Precision.HIGHEST)

    ways = migrant_slot.shape[2]
    width = migrant_slot.shape[3]
    slots = migrant_slot.reshape(-1, lanes)
    keep = jnp.arange(width, dtype=jnp.int32)[None, :] < migrant_count.reshape(ways, 1)
    keep = keep.astype(f32).reshape(-1, lanes)
    early = jnp.stack(
        [
            positions[0] * live,
            positions[1] * live,
            velocity[0] * live,
            velocity[1] * live,
            density * live,
            live_mass,
        ]
    )
    still = pick(slots, keep, early.reshape(-1, blocks, lanes), ways)

    late, peak = halo_forces(
        halo_count, halo, fields, own, windage.reshape(2, blocks, lanes), rows, cols
    )
    peaks = jnp.sqrt(everywhere_max(peak))
    delta_t = time_step(peaks[0], peaks[1])
    moving = pick(slots, keep, late, ways)
    came = jnp.stack(send_on(jnp.concatenate([still, moving])))

    acceleration = late[:2].reshape(2, rows, cols, lanes)
    rate = late[2].reshape(rows, cols, lanes)
    new_velocity = (velocity + delta_t * acceleration) * live[None]
    new_position = (positions + delta_t * new_velocity) * live[None]
    new_density = (density + delta_t * rate) * live
    state_next = jnp.concatenate([new_position, new_velocity, new_density[None], acceleration])

    moved_velocity = came[:, 2:4] + delta_t * came[:, 6:8]
    moved_position = came[:, 0:2] + delta_t * moved_velocity
    moved_density = came[:, 4:5] + delta_t * came[:, 8:9]
    arrivals = jnp.concatenate(
        [moved_position, moved_velocity, moved_density, came[:, 5:6], came[:, 6:8]], axis=1
    )
    return (state_next, arrivals.reshape(1, 1, ways, arrivals.shape[1], width))


def solution(mesh):
    in_specs = (
        P(None, "shore", "cross", None),
        P(None, "shore", "cross", None),
        P("shore", "cross", None),
        P("shore", "cross", None),
        P("shore", "cross"),
        P("shore", "cross", None),
        P(),
        P("shore", "cross", None, None),
        P("shore", "cross", None),
    )
    out_specs = (P(None, "shore", "cross", None), P("shore", "cross", None, None, None))
    return jax.shard_map(body, mesh=mesh, in_specs=in_specs, out_specs=out_specs, check_vma=False)
```
